32 devices in a mesh: row: 4 (over y, x), col: 8 (over z, core).
Axes of the slice: x: 2, y: 2, z: 4, core: 2. Of those that a mesh axis runs over, the one named last changes fastest.
Arguments:
- orbitals: bfloat16 [16384, 1024], P('row', 'col'), may hold values from -0.1875 to 0.1875
- kernel: bfloat16 [16384, 16384], P('col', 'row'), may hold values from -6 to 6
- applied: bfloat16 [16384, 256], P('col', 'row'), may hold values from -1.5 to 1.5
- fit: bfloat16 [16384, 16384], P('row', 'col'), may hold values from -0.046875 to 0.046875
Outputs:
- exchange_term: bfloat16 [256, 16384], P('row', 'col')
The draws below stay inside these ranges and needn't reach their ends.
All inputs are finite; a program needn't handle non-finite values.
Results may differ from the reference program's by a relative error of at most 0.0058.
Values may be sent and summed in bfloat16 or wider, within the bound.
A program may use at most 128 MiB of HBM per device.

```python
import jax
import jax.numpy as jnp
from jax import lax

NORB = 1024
NMU = 16384
NAPP = 256
NG = 16384
N_COL = 8


def shard_levels(own_key, dims, split, low, top_value):
    factor_of = 1.0
    for dim, blocks in split:
        draws = jax.random.uniform(jax.random.fold_in(jax.random.fold_in(own_key, 6), dim), (blocks,), jnp.float32, low / len(split), top_value / len(split))
        factor_of = factor_of * jnp.repeat(jnp.exp(draws), dims[dim] // blocks).reshape((-1,) + (1,) * (len(dims) - 1 - dim))
    return factor_of


def bell_draw(stream_key, shape, spread, bound, split=(), dtype=jnp.bfloat16):
    values = jax.random.normal(stream_key, shape, jnp.float32) * spread
    if len(split) > 0:
        values = shard_levels(stream_key, shape, split, -0.22, 0.18) * values
    return jnp.clip(values, min=-bound, max=bound).astype(dtype)


def setup_inputs(seed: int = 0) -> dict:
    key_of = jax.random.split(jax.random.key(seed), 5)
    return {
        "orbitals": bell_draw(key_of[0], (NMU, NORB), NORB ** -0.5, 0.1875, ((0, 4), (1, 8))),
        "kernel": bell_draw(key_of[1], (NMU, NMU), 1.0, 6.0, ((0, 8), (1, 4))),
        "applied": bell_draw(key_of[2], (NMU, NAPP), 0.25, 1.5, ((0, 8), (1, 4))),
        "fit": bell_draw(key_of[3], (NMU, NG), NMU ** -0.5, 0.046875, ((0, 4), (1, 8))),
    }


def reference(orbitals, kernel, applied, fit):
    blocks = N_COL
    width = NMU // blocks
    orb_blocks = orbitals.reshape(blocks, width, NORB)
    kernel_blocks = kernel.reshape(blocks, width, NMU)
    applied_blocks = applied.reshape(blocks, width, NAPP)

    def accumulate(projected, items):
        orb_part, kernel_part, applied_part = items
        density = jnp.dot(orb_part, orbitals.T, preferred_element_type=jnp.float32)
        weighted = (density * kernel_part.astype(jnp.float32)).astype(jnp.bfloat16)
        return projected + jnp.dot(weighted.T, applied_part, preferred_element_type=jnp.float32), None

    projected, _ = lax.scan(accumulate, jnp.zeros((NMU, NAPP), jnp.float32), (orb_blocks, kernel_blocks, applied_blocks))
    projected_low = projected.astype(jnp.bfloat16)
    result = jnp.dot(projected_low.T, fit, preferred_element_type=jnp.float32)
    return (-result).astype(jnp.bfloat16)
```

```python
import functools

import jax
import jax.numpy as jnp
from jax import lax
from jax.experimental import pallas as pl
from jax.experimental.pallas import tpu as pltpu
from jax.sharding import PartitionSpec as P

MESH = pl.DeviceIdType.MESH
H = 8


def gather_kernel(R, C, orb, at, kern, pt, obuf, cbuf, abuf, kbuf,
                  loc_s, kern_s, up_s, dn_s, sib_s, pl_s, line_r, sib_r, pl_r, a_s, a_r):
    Z = C // 2
    N, B = orb.shape
    NU, M = kern.shape
    J = at.shape[0]
    RS = N // H
    HH = H // 2
    r = lax.axis_index("row")
    c = lax.axis_index("col")
    z = c // 2
    k = c % 2
    sib = c + 1 - 2 * k
    xn = r + 1 - 2 * (r % 2)
    yn = (r + 2) % 4
    diag = r == z
    dx = (r % 2) != (z % 2)
    dy = (r // 2) != (z // 2)

    kcopy = pltpu.make_async_copy(kern, kbuf, kern_s)
    kcopy.start()

    def lanes(kk):
        return pl.ds(pl.multiple_of(kk * B, B), B)

    own = pltpu.make_async_copy(orb, obuf.at[z, :, lanes(k)], loc_s)
    own.start()

    barrier = pltpu.get_barrier_semaphore()
    for o in range(R):
        for kk in range(2):
            if o == 0 and kk == 1:
                continue
            dst = sib if o == 0 else 2 * z + kk
            pl.semaphore_signal(barrier, inc=1, device_id=((r + o) % R, dst), device_id_type=MESH)

    @pl.when(z > 0)
    def _():
        pl.semaphore_signal(barrier, inc=1, device_id=(r, c - 2), device_id_type=MESH)

    @pl.when(z < Z - 1)
    def _():
        pl.semaphore_signal(barrier, inc=1, device_id=(r, c + 2), device_id_type=MESH)

    pl.semaphore_wait(barrier, 2 * R - 1 + jnp.where(z > 0, 1, 0) + jnp.where(z < Z - 1, 1, 0))
    own.wait()

    def rows(q):
        return pl.ds(pl.multiple_of((q % 2) * (N // 2) + (q // 2) * RS, RS), RS)

    def crows(f):
        return pl.ds(pl.multiple_of(f * RS, RS), RS)

    def line(zp, q, up):
        ref = obuf.at[zp, rows(q), lanes(k)]
        return pltpu.make_async_remote_copy(
            ref, ref, (up_s if up else dn_s).at[zp, q], line_r.at[zp, q],
            device_id=(r, c + 2 if up else c - 2), device_id_type=MESH)

    def sibling(zp, q, kk):
        ref = obuf.at[zp, rows(q), lanes(kk)]
        return pltpu.make_async_remote_copy(
            ref, ref, sib_s.at[zp, q], sib_r.at[zp, q], device_id=(r, sib), device_id_type=MESH)

    def from_diag(zp, q):
        path = (q // 2) % 2
        return pltpu.make_async_remote_copy(
            obuf.at[zp, rows(q), lanes(k)], cbuf.at[zp, crows(q // 2), lanes(k)],
            pl_s.at[zp, q], pl_r.at[zp, k, q // 2],
            device_id=(jnp.where(path == 0, xn, yn), 2 * z + q % 2), device_id_type=MESH)

    def relay(zp, kk, f):
        path = f % 2
        ref = cbuf.at[zp, crows(f), lanes(kk)]
        last = (path == 0) == dx
        to = jnp.where(path == 0, jnp.where(dy, xn, yn), jnp.where(dx, yn, xn))
        return pltpu.make_async_remote_copy(
            ref, ref, pl_s.at[zp, 2 * f + kk], pl_r.at[zp, kk, f],
            device_id=(to, c), device_id_type=MESH)

    def relays(f):
        path = f % 2
        return jnp.where(path == 0, dx, dy)

    def acopy(o):
        return pltpu.make_async_remote_copy(
            at, abuf.at[pl.ds(pl.multiple_of(r * J, J), J)], a_s.at[o], a_r.at[o],
            device_id=((r + o) % R, c), device_id_type=MESH)

    def do_relay(zp, f):
        @pl.when(jnp.logical_not(diag))
        def _():
            for kk in range(2):
                desc = relay(zp, kk, f)
                desc.wait_recv()

                @pl.when(relays(f))
                def _():
                    desc.start()

    def spread(zp, q, up, down):
        if up:
            @pl.when(z < Z - 1)
            def _():
                line(zp, q, True).start()
        if down:
            @pl.when(z > 0)
            def _():
                line(zp, q, False).start()
        sibling(zp, q, k).start()

        @pl.when(diag)
        def _():
            from_diag(zp, q).start()

    @pl.loop(0, H)
    def _(q):
        spread(z, q, True, True)

    for o in range(1, R):
        acopy(o).start()
    acp = pltpu.make_async_copy(at, abuf.at[pl.ds(pl.multiple_of(r * J, J), J)], a_s.at[0])
    acp.start()

    @pl.loop(0, HH)
    def _(f):
        do_relay(z, f)

    for d in range(1, Z):
        below = z - d >= 0
        above = z + d < Z

        @pl.loop(0, H)
        def _(q):
            @pl.when(below)
            def _():
                line(z - d, q, True).wait_recv()
                spread(z - d, q, True, False)

            @pl.when(above)
            def _():
                line(z + d, q, False).wait_recv()
                spread(z + d, q, False, True)

            @pl.when((q % 2 == 1) & (q > 1))
            def _():
                @pl.when(below)
                def _():
                    do_relay(z - d, q // 2 - 1)

                @pl.when(above)
                def _():
                    do_relay(z + d, q // 2 - 1)

        @pl.when(below)
        def _():
            do_relay(z - d, HH - 1)

        @pl.when(above)
        def _():
            do_relay(z + d, HH - 1)

    @pl.loop(0, Z)
    def _(zp):
        @pl.loop(0, H)
        def _(q):
            sibling(zp, q, 1 - k).wait_recv()

    half = pl.ds(pl.multiple_of(k * (N // 2), N // 2), N // 2)

    @pl.when(diag)
    def _():
        cp = pltpu.make_async_copy(obuf.at[:, half], cbuf, loc_s)
        cp.start()
        cp.wait()

    acp.wait()
    for o in range(1, R):
        acopy(o).wait_recv()
    kcopy.wait()

    T = 512
    S = 512

    @pl.loop(0, M // T)
    def _(t):
        mu = pl.ds(pl.multiple_of(t * T, T), T)
        total = jnp.zeros((abuf.shape[0], T), jnp.float32)
        for n in range(NU // S):
            nu = pl.ds(n * S, S)
            dens = jnp.zeros((S, T), jnp.float32)
            for zp in range(Z):
                dens += lax.dot_general(cbuf[zp, nu], obuf[zp, mu], (((1,), (1,)), ((), ())),
                                        preferred_element_type=jnp.float32)
            w = (dens * kbuf[nu, mu].astype(jnp.float32)).astype(jnp.bfloat16)
            total += jnp.dot(abuf[:, nu], w, preferred_element_type=jnp.float32)
        pt[:, mu] = total

    for o in range(1, R):
        acopy(o).wait_send()

    @pl.loop(0, Z)
    def _(zp):
        @pl.loop(0, H)
        def _(q):
            @pl.when((zp <= z) & (z < Z - 1))
            def _():
                line(zp, q, True).wait_send()

            @pl.when((zp >= z) & (z > 0))
            def _():
                line(zp, q, False).wait_send()

            sibling(zp, q, k).wait_send()

            @pl.when(diag)
            def _():
                from_diag(zp, q).wait_send()

            @pl.when(jnp.logical_not(diag) & relays(q // 2))
            def _():
                relay(zp, q % 2, q // 2).wait_send()


def projected_part(R, C, orbitals, kernel, applied):
    Z = C // 2
    N, B = orbitals.shape
    NU, M = kernel.shape
    at = applied.T
    J = at.shape[0]
    dma = pltpu.SemaphoreType.DMA
    return pl.pallas_call(
        functools.partial(gather_kernel, R, C),
        out_shape=jax.ShapeDtypeStruct((R * J, M), jnp.float32),
        in_specs=[pl.BlockSpec(memory_space=pl.ANY)] * 3,
        out_specs=pl.BlockSpec(memory_space=pltpu.VMEM),
        scratch_shapes=[
            pltpu.VMEM((Z, N, 2 * B), jnp.bfloat16),
            pltpu.VMEM((Z, NU, 2 * B), jnp.bfloat16),
            pltpu.VMEM((R * J, NU), jnp.bfloat16),
            pltpu.VMEM((NU, M), jnp.bfloat16),
            dma, dma,
            dma((Z, H)), dma((Z, H)), dma((Z, H)), dma((Z, H)),
            dma((Z, H)), dma((Z, H)), dma((Z, 2, H // 2)),
            dma((R,)), dma((R,)),
        ],
        compiler_params=pltpu.CompilerParams(
            collective_id=0, has_side_effects=True, vmem_limit_bytes=60 * 1024 * 1024),
    )(orbitals, at, kernel)


def plain(orbitals, kernel, applied, fit):
    columns = lax.all_gather(orbitals, "row", axis=0, tiled=True)
    nearby = lax.all_to_all(columns, "col", split_axis=0, concat_axis=1, tiled=True)
    density = lax.dot_general(
        nearby,
        lax.all_gather(orbitals, "col", axis=1, tiled=True),
        (((1,), (1,)), ((), ())),
        preferred_element_type=jnp.float32,
    )
    weighted = (density * kernel.astype(jnp.float32)).astype(jnp.bfloat16)
    partial_sum = lax.dot_general(
        weighted,
        lax.all_gather(applied, "row", axis=1, tiled=True),
        (((0,), (0,)), ((), ())),
        preferred_element_type=jnp.float32,
    )
    projected = lax.psum(partial_sum, "col")
    projected_low = projected.astype(jnp.bfloat16)
    result = lax.psum_scatter(
        -lax.dot_general(
            projected_low, fit, (((0,), (0,)), ((), ())), preferred_element_type=jnp.float32
        ),
        "row",
        scatter_dimension=0,
        tiled=True,
    )
    return result.astype(jnp.bfloat16)


def relayed(R, C, orbitals, kernel, applied, fit):
    partial_sum = projected_part(R, C, orbitals, kernel, applied)
    projected = lax.psum(partial_sum, "col")
    result = lax.psum_scatter(
        -jnp.dot(projected.astype(jnp.bfloat16), fit, preferred_element_type=jnp.float32),
        "row",
        scatter_dimension=0,
        tiled=True,
    )
    return result.astype(jnp.bfloat16)


def solution(mesh):
    R, C = mesh.shape["row"], mesh.shape["col"]

    def per_device(orbitals, kernel, applied, fit):
        if R == 4 and C == 2 * R and orbitals.shape[1] % 128 == 0:
            return relayed(R, C, orbitals, kernel, applied, fit)
        return plain(orbitals, kernel, applied, fit)

    return jax.shard_map(
        per_device,
        mesh=mesh,
        in_specs=(P("row", "col"), P("col", "row"), P("col", "row"), P("row", "col")),
        out_specs=P("row", "col"),
        check_vma=False,
    )
```

```python
import functools

import jax
import jax.numpy as jnp
from jax import lax
from jax.experimental import pallas as pl
from jax.experimental.pallas import tpu as pltpu
from jax.sharding import PartitionSpec as P

MESH = pl.DeviceIdType.MESH
H = 8
T = 512
S = 512
KS = 4


def whole_kernel(R, C, orb, at, kern, fit, out, obuf, cbuf, abuf, kbuf, fbuf,
                 pown, sout, sin, upin, upout, dnin, dnout, tot, acc, rout, rin,
                 loc_s, kern_s, fit_s, up_s, dn_s, sib_s, pl_s, line_r, sib_r, pl_r, a_s, a_r,
                 pair_s, pair_r, pre_s, pre_r, suf_s, suf_r, tot_s, tot_r, red_s, red_r):
    Z = C // 2
    N, B = orb.shape
    NU, M = kern.shape
    J = at.shape[0]
    RS = N // H
    HH = H // 2
    r = lax.axis_index("row")
    c = lax.axis_index("col")
    z = c // 2
    k = c % 2
    sib = c + 1 - 2 * k
    xn = r + 1 - 2 * (r % 2)
    yn = (r + 2) % 4
    diag = r == z
    dx = (r % 2) != (z % 2)
    dy = (r // 2) != (z // 2)

    NT = M // T
    W = T // 2

    def ktile(t):
        return pltpu.make_async_copy(
            kern.at[:, pl.ds(pl.multiple_of(t * T, T), T)], kbuf.at[t % KS], kern_s.at[t % KS])

    for t in range(min(KS, NT)):
        ktile(t).start()
    fcopy = pltpu.make_async_copy(fit, fbuf, fit_s)
    fcopy.start()

    @pl.when(z == 0)
    def _():
        upin[...] = jnp.zeros_like(upin)

    @pl.when(z == Z - 1)
    def _():
        dnin[...] = jnp.zeros_like(dnin)
    acc[...] = jnp.zeros_like(acc)

    def lanes(kk):
        return pl.ds(pl.multiple_of(kk * B, B), B)

    own = pltpu.make_async_copy(orb, obuf.at[z, :, lanes(k)], loc_s)
    own.start()

    barrier = pltpu.get_barrier_semaphore()
    for o in range(R):
        for kk in range(2):
            if o == 0 and kk == 1:
                continue
            dst = sib if o == 0 else 2 * z + kk
            pl.semaphore_signal(barrier, inc=1, device_id=((r + o) % R, dst), device_id_type=MESH)

    @pl.when(z > 0)
    def _():
        pl.semaphore_signal(barrier, inc=1, device_id=(r, c - 2), device_id_type=MESH)

    @pl.when(z < Z - 1)
    def _():
        pl.semaphore_signal(barrier, inc=1, device_id=(r, c + 2), device_id_type=MESH)

    pl.semaphore_wait(barrier, 2 * R - 1 + jnp.where(z > 0, 1, 0) + jnp.where(z < Z - 1, 1, 0))
    own.wait()

    def rows(q):
        return pl.ds(pl.multiple_of((q % 2) * (N // 2) + (q // 2) * RS, RS), RS)

    def crows(f):
        return pl.ds(pl.multiple_of(f * RS, RS), RS)

    def line(zp, q, up):
        ref = obuf.at[zp, rows(q), lanes(k)]
        return pltpu.make_async_remote_copy(
            ref, ref, (up_s if up else dn_s).at[zp, q], line_r.at[zp, q],
            device_id=(r, c + 2 if up else c - 2), device_id_type=MESH)

    def sibling(zp, q, kk):
        ref = obuf.at[zp, rows(q), lanes(kk)]
        return pltpu.make_async_remote_copy(
            ref, ref, sib_s.at[zp, q], sib_r.at[zp, q], device_id=(r, sib), device_id_type=MESH)

    def from_diag(zp, q):
        path = (q // 2) % 2
        return pltpu.make_async_remote_copy(
            obuf.at[zp, rows(q), lanes(k)], cbuf.at[zp, crows(q // 2), lanes(k)],
            pl_s.at[zp, q], pl_r.at[zp, k, q // 2],
            device_id=(jnp.where(path == 0, xn, yn), 2 * z + q % 2), device_id_type=MESH)

    def relay(zp, kk, f):
        path = f % 2
        ref = cbuf.at[zp, crows(f), lanes(kk)]
        last = (path == 0) == dx
        to = jnp.where(path == 0, jnp.where(dy, xn, yn), jnp.where(dx, yn, xn))
        return pltpu.make_async_remote_copy(
            ref, ref, pl_s.at[zp, 2 * f + kk], pl_r.at[zp, kk, f],
            device_id=(to, c), device_id_type=MESH)

    def relays(f):
        path = f % 2
        return jnp.where(path == 0, dx, dy)

    def acopy(o):
        return pltpu.make_async_remote_copy(
            at, abuf.at[pl.ds(pl.multiple_of(r * J, J), J)], a_s.at[o], a_r.at[o],
            device_id=((r + o) % R, c), device_id_type=MESH)

    def do_relay(zp, f):
        @pl.when(jnp.logical_not(diag))
        def _():
            for kk in range(2):
                desc = relay(zp, kk, f)
                desc.wait_recv()

                @pl.when(relays(f))
                def _():
                    desc.start()

    def spread(zp, q, up, down):
        if up:
            @pl.when(z < Z - 1)
            def _():
                line(zp, q, True).start()
        if down:
            @pl.when(z > 0)
            def _():
                line(zp, q, False).start()
        sibling(zp, q, k).start()

        @pl.when(diag)
        def _():
            from_diag(zp, q).start()

    @pl.loop(0, H)
    def _(q):
        spread(z, q, True, True)

    for o in range(1, R):
        acopy(o).start()
    acp = pltpu.make_async_copy(at, abuf.at[pl.ds(pl.multiple_of(r * J, J), J)], a_s.at[0])
    acp.start()

    @pl.loop(0, HH)
    def _(f):
        do_relay(z, f)

    for d in range(1, Z):
        below = z - d >= 0
        above = z + d < Z

        @pl.loop(0, H)
        def _(q):
            @pl.when(below)
            def _():
                line(z - d, q, True).wait_recv()
                spread(z - d, q, True, False)

            @pl.when(above)
            def _():
                line(z + d, q, False).wait_recv()
                spread(z + d, q, False, True)

            @pl.when((q % 2 == 1) & (q > 1))
            def _():
                @pl.when(below)
                def _():
                    do_relay(z - d, q // 2 - 1)

                @pl.when(above)
                def _():
                    do_relay(z + d, q // 2 - 1)

        @pl.when(below)
        def _():
            do_relay(z - d, HH - 1)

        @pl.when(above)
        def _():
            do_relay(z + d, HH - 1)

    @pl.loop(0, Z)
    def _(zp):
        @pl.loop(0, H)
        def _(q):
            sibling(zp, q, 1 - k).wait_recv()

    half = pl.ds(pl.multiple_of(k * (N // 2), N // 2), N // 2)

    @pl.when(diag)
    def _():
        cp = pltpu.make_async_copy(obuf.at[:, half], cbuf, loc_s)
        cp.start()
        cp.wait()

    acp.wait()
    for o in range(1, R):
        acopy(o).wait_recv()

    def pair(t):
        return pltpu.make_async_remote_copy(
            sout.at[t], sin.at[t], pair_s.at[t], pair_r.at[t], device_id=(r, sib), device_id_type=MESH)

    def prefix(t):
        return pltpu.make_async_remote_copy(
            upout.at[t], upin.at[t], pre_s.at[t], pre_r.at[t], device_id=(r, c + 2), device_id_type=MESH)

    def suffix(t):
        return pltpu.make_async_remote_copy(
            dnout.at[t], dnin.at[t], suf_s.at[t], suf_r.at[t], device_id=(r, c - 2), device_id_type=MESH)

    def share(t, kk):
        ref = tot.at[t, :, pl.ds(pl.multiple_of(kk * W, W), W)]
        return pltpu.make_async_remote_copy(
            ref, ref, tot_s.at[t], tot_r.at[t], device_id=(r, sib), device_id_type=MESH)

    def project(t):
        ktile(t).wait()
        mu = pl.ds(pl.multiple_of(t * T, T), T)
        total = jnp.zeros((abuf.shape[0], T), jnp.float32)
        for n in range(NU // S):
            nu = pl.ds(n * S, S)
            dens = jnp.zeros((S, T), jnp.float32)
            for zp in range(Z):
                dens += lax.dot_general(cbuf[zp, nu], obuf[zp, mu], (((1,), (1,)), ((), ())),
                                        preferred_element_type=jnp.float32)
            w = (dens * kbuf[t % KS, nu].astype(jnp.float32)).astype(jnp.bfloat16)
            total += jnp.dot(abuf[:, nu], w, preferred_element_type=jnp.float32)
        first, second = total[:, :W], total[:, W:]
        pown[t] = jnp.where(k == 0, first, second)
        sout[t] = jnp.where(k == 0, second, first).astype(jnp.bfloat16)
        pair(t).start()

        @pl.when(t + KS < NT)
        def _():
            ktile(t + KS).start()

    far = jnp.maximum(z, Z - 1 - z)

    @pl.loop(0, NT + Z + 1)
    def _(s):
        @pl.when(s < NT)
        def _():
            project(s)

        t_pair = s - 1

        @pl.when((t_pair >= 0) & (t_pair < NT))
        def _():
            pair(t_pair).wait_recv()
            pown[t_pair] += sin[t_pair].astype(jnp.float32)

        t_up = s - 1 - z

        @pl.when((t_up >= 0) & (t_up < NT))
        def _():
            @pl.when(z > 0)
            def _():
                prefix(t_up).wait_recv()

            @pl.when(z < Z - 1)
            def _():
                upout[t_up] = (pown[t_up] + upin[t_up].astype(jnp.float32)).astype(jnp.bfloat16)
                prefix(t_up).start()

        t_dn = s - 1 - (Z - 1 - z)

        @pl.when((t_dn >= 0) & (t_dn < NT))
        def _():
            @pl.when(z < Z - 1)
            def _():
                suffix(t_dn).wait_recv()

            @pl.when(z > 0)
            def _():
                dnout[t_dn] = (pown[t_dn] + dnin[t_dn].astype(jnp.float32)).astype(jnp.bfloat16)
                suffix(t_dn).start()

        t_tot = s - 1 - far

        @pl.when((t_tot >= 0) & (t_tot < NT))
        def _():
            tot[t_tot, :, pl.ds(pl.multiple_of(k * W, W), W)] = (
                pown[t_tot] + upin[t_tot].astype(jnp.float32) + dnin[t_tot].astype(jnp.float32)
            ).astype(jnp.bfloat16)
            share(t_tot, k).start()

        t_ex = s - 2 - far

        @pl.when((t_ex >= 0) & (t_ex < NT))
        def _():
            share(t_ex, 1 - k).wait_recv()

            @pl.when(t_ex == 0)
            def _():
                fcopy.wait()
            acc[...] += jnp.dot(
                tot[t_ex], fbuf[pl.ds(pl.multiple_of(t_ex * T, T), T)], preferred_element_type=jnp.float32)

    def quarter(o):
        return pltpu.make_async_remote_copy(
            rout.at[o - 1], rin.at[o - 1], red_s.at[o - 1], red_r.at[o - 1],
            device_id=((r + o) % R, c), device_id_type=MESH)

    def rows_of(rr):
        return pl.ds(pl.multiple_of(rr * J, J), J)

    for o in (2, 1, 3)[: R - 1]:
        rout[o - 1] = acc[rows_of((r + o) % R)].astype(jnp.bfloat16)
        quarter(o).start()
    result = acc[rows_of(r)]
    for o in range(1, R):
        quarter(o).wait_recv()
        result += rin[o - 1].astype(jnp.float32)
    out[...] = (-result).astype(jnp.bfloat16)

    for o in range(1, R):
        acopy(o).wait_send()
        quarter(o).wait_send()

    @pl.loop(0, NT)
    def _(t):
        pair(t).wait_send()
        share(t, k).wait_send()

        @pl.when(z < Z - 1)
        def _():
            prefix(t).wait_send()

        @pl.when(z > 0)
        def _():
            suffix(t).wait_send()

    @pl.loop(0, Z)
    def _(zp):
        @pl.loop(0, H)
        def _(q):
            @pl.when((zp <= z) & (z < Z - 1))
            def _():
                line(zp, q, True).wait_send()

            @pl.when((zp >= z) & (z > 0))
            def _():
                line(zp, q, False).wait_send()

            sibling(zp, q, k).wait_send()

            @pl.when(diag)
            def _():
                from_diag(zp, q).wait_send()

            @pl.when(jnp.logical_not(diag) & relays(q // 2))
            def _():
                relay(zp, q % 2, q // 2).wait_send()


def relayed(R, C, orbitals, kernel, applied, fit):
    Z = C // 2
    N, B = orbitals.shape
    NU, M = kernel.shape
    G = fit.shape[1]
    at = applied.T
    J = at.shape[0]
    NT = M // T
    W = T // 2
    dma = pltpu.SemaphoreType.DMA
    low, high = jnp.bfloat16, jnp.float32
    tiles = pltpu.VMEM((NT, R * J, W), low)
    return pl.pallas_call(
        functools.partial(whole_kernel, R, C),
        out_shape=jax.ShapeDtypeStruct((J, G), low),
        in_specs=[pl.BlockSpec(memory_space=pl.ANY)] * 4,
        out_specs=pl.BlockSpec(memory_space=pltpu.VMEM),
        scratch_shapes=[
            pltpu.VMEM((Z, N, 2 * B), low),
            pltpu.VMEM((Z, NU, 2 * B), low),
            pltpu.VMEM((R * J, NU), low),
            pltpu.VMEM((KS, NU, T), low),
            pltpu.VMEM((M, G), low),
            pltpu.VMEM((NT, R * J, W), high),
            tiles, tiles, tiles, tiles, tiles, tiles,
            pltpu.VMEM((NT, R * J, T), low),
            pltpu.VMEM((R * J, G), high),
            pltpu.VMEM((R - 1, J, G), low),
            pltpu.VMEM((R - 1, J, G), low),
            dma, dma((KS,)), dma,
            dma((Z, H)), dma((Z, H)), dma((Z, H)), dma((Z, H)),
            dma((Z, H)), dma((Z, H)), dma((Z, 2, H // 2)),
            dma((R,)), dma((R,)),
        ] + [dma((NT,))] * 8 + [dma((R - 1,))] * 2,
        compiler_params=pltpu.CompilerParams(
            collective_id=0, has_side_effects=True, vmem_limit_bytes=60 * 1024 * 1024),
    )(orbitals, at, kernel, fit)


def plain(orbitals, kernel, applied, fit):
    columns = lax.all_gather(orbitals, "row", axis=0, tiled=True)
    nearby = lax.all_to_all(columns, "col", split_axis=0, concat_axis=1, tiled=True)
    density = lax.dot_general(
        nearby,
        lax.all_gather(orbitals, "col", axis=1, tiled=True),
        (((1,), (1,)), ((), ())),
        preferred_element_type=jnp.float32,
    )
    weighted = (density * kernel.astype(jnp.float32)).astype(jnp.bfloat16)
    partial_sum = lax.dot_general(
        weighted,
        lax.all_gather(applied, "row", axis=1, tiled=True),
        (((0,), (0,)), ((), ())),
        preferred_element_type=jnp.float32,
    )
    projected = lax.psum(partial_sum, "col")
    projected_low = projected.astype(jnp.bfloat16)
    result = lax.psum_scatter(
        -lax.dot_general(
            projected_low, fit, (((0,), (0,)), ((), ())), preferred_element_type=jnp.float32
        ),
        "row",
        scatter_dimension=0,
        tiled=True,
    )
    return result.astype(jnp.bfloat16)


def solution(mesh):
    R, C = mesh.shape["row"], mesh.shape["col"]

    def per_device(orbitals, kernel, applied, fit):
        if R == 4 and C == 2 * R and orbitals.shape[1] % 128 == 0:
            return relayed(R, C, orbitals, kernel, applied, fit)
        return plain(orbitals, kernel, applied, fit)

    return jax.shard_map(
        per_device,
        mesh=mesh,
        in_specs=(P("row", "col"), P("col", "row"), P("col", "row"), P("row", "col")),
        out_specs=P("row", "col"),
        check_vma=False,
    )
```

```python
import functools

import jax
import jax.numpy as jnp
from jax import lax
from jax.experimental import pallas as pl
from jax.experimental.pallas import tpu as pltpu
from jax.sharding import PartitionSpec as P

MESH = pl.DeviceIdType.MESH
H = 8
T = 512
S = 512
KS = 4


def whole_kernel(R, C, orb, at, kern, fit, out, obuf, cbuf, abuf, kbuf, fbuf,
                 pown, sout, sin, upin, upout, dnin, dnout, tot, acc, rout, rin,
                 loc_s, kern_s, fit_s, up_s, dn_s, sib_s, pl_s, line_r, sib_r, pl_r, a_s, a_r,
                 pair_s, pair_r, pre_s, pre_r, suf_s, suf_r, tot_s, tot_r, red_s, red_r):
    Z = C // 2
    N, B = orb.shape
    NU, M = kern.shape
    J = at.shape[0]
    RS = N // H
    HH = H // 2
    r = lax.axis_index("row")
    c = lax.axis_index("col")
    z = c // 2
    k = c % 2
    sib = c + 1 - 2 * k
    xn = r + 1 - 2 * (r % 2)
    yn = (r + 2) % 4
    diag = r == z
    dx = (r % 2) != (z % 2)
    dy = (r // 2) != (z // 2)

    NT = M // T
    W = T // 2

    def ktile(t):
        return pltpu.make_async_copy(
            kern.at[:, pl.ds(pl.multiple_of(t * T, T), T)], kbuf.at[t % KS], kern_s.at[t % KS])

    for t in range(min(KS, NT)):
        ktile(t).start()
    fcopy = pltpu.make_async_copy(fit, fbuf, fit_s)
    fcopy.start()

    @pl.when(z == 0)
    def _():
        upin[...] = jnp.zeros_like(upin)

    @pl.when(z == Z - 1)
    def _():
        dnin[...] = jnp.zeros_like(dnin)
    acc[...] = jnp.zeros_like(acc)

    def lanes(kk):
        return pl.ds(pl.multiple_of(kk * B, B), B)

    own = pltpu.make_async_copy(orb, obuf.at[z, :, lanes(k)], loc_s)
    own.start()

    barrier = pltpu.get_barrier_semaphore()
    for o in range(R):
        for kk in range(2):
            if o == 0 and kk == 1:
                continue
            dst = sib if o == 0 else 2 * z + kk
            pl.semaphore_signal(barrier, inc=1, device_id=((r + o) % R, dst), device_id_type=MESH)

    @pl.when(z > 0)
    def _():
        pl.semaphore_signal(barrier, inc=1, device_id=(r, c - 2), device_id_type=MESH)

    @pl.when(z < Z - 1)
    def _():
        pl.semaphore_signal(barrier, inc=1, device_id=(r, c + 2), device_id_type=MESH)

    pl.semaphore_wait(barrier, 2 * R - 1 + jnp.where(z > 0, 1, 0) + jnp.where(z < Z - 1, 1, 0))
    own.wait()

    def rows(q):
        return pl.ds(pl.multiple_of((q % 2) * (N // 2) + (q // 2) * RS, RS), RS)

    def crows(f):
        return pl.ds(pl.multiple_of(f * RS, RS), RS)

    def line(zp, q, up):
        ref = obuf.at[zp, rows(q), lanes(k)]
        return pltpu.make_async_remote_copy(
            ref, ref, (up_s if up else dn_s).at[zp, q], line_r.at[zp, q],
            device_id=(r, c + 2 if up else c - 2), device_id_type=MESH)

    def sibling(zp, q, kk):
        ref = obuf.at[zp, rows(q), lanes(kk)]
        return pltpu.make_async_remote_copy(
            ref, ref, sib_s.at[zp, q], sib_r.at[zp, q], device_id=(r, sib), device_id_type=MESH)

    def from_diag(zp, q):
        path = (q // 2) % 2
        return pltpu.make_async_remote_copy(
            obuf.at[zp, rows(q), lanes(k)], cbuf.at[zp, crows(q // 2), lanes(k)],
            pl_s.at[zp, q], pl_r.at[zp, k, q // 2],
            device_id=(jnp.where(path == 0, xn, yn), 2 * z + q % 2), device_id_type=MESH)

    def relay(zp, kk, f):
        path = f % 2
        ref = cbuf.at[zp, crows(f), lanes(kk)]
        to = jnp.where(path == 0, jnp.where(dy, xn, yn), jnp.where(dx, yn, xn))
        return pltpu.make_async_remote_copy(
            ref, ref, pl_s.at[zp, 2 * f + kk], pl_r.at[zp, kk, f],
            device_id=(to, c), device_id_type=MESH)

    def relays(f):
        path = f % 2
        return jnp.where(path == 0, dx, dy)

    def acopy(o):
        return pltpu.make_async_remote_copy(
            at, abuf.at[pl.ds(pl.multiple_of(r * J, J), J)], a_s.at[o], a_r.at[o],
            device_id=((r + o) % R, c), device_id_type=MESH)

    def do_relay(zp, f):
        @pl.when(jnp.logical_not(diag) & relays(f))
        def _():
            for kk in range(2):
                desc = relay(zp, kk, f)
                desc.wait_recv()
                desc.start()

    def spread(zp, q, up, down):
        if up:
            @pl.when(z < Z - 1)
            def _():
                line(zp, q, True).start()
        if down:
            @pl.when(z > 0)
            def _():
                line(zp, q, False).start()
        sibling(zp, q, k).start()

        @pl.when(diag)
        def _():
            from_diag(zp, q).start()

    @pl.loop(0, H)
    def _(q):
        spread(z, q, True, True)

    for o in range(1, R):
        acopy(o).start()
    acp = pltpu.make_async_copy(at, abuf.at[pl.ds(pl.multiple_of(r * J, J), J)], a_s.at[0])
    acp.start()

    def relay_step(d, f):
        if d == 0:
            do_relay(z, f)
            return

        @pl.when(z - d >= 0)
        def _():
            do_relay(z - d, f)

        @pl.when(z + d < Z)
        def _():
            do_relay(z + d, f)

    for d in range(1, Z):
        @pl.loop(0, H)
        def _(q):
            @pl.when(z - d >= 0)
            def _():
                line(z - d, q, True).wait_recv()
                spread(z - d, q, True, False)

            @pl.when(z + d < Z)
            def _():
                line(z + d, q, False).wait_recv()
                spread(z + d, q, False, True)

            @pl.when(q % 2 == 1)
            def _():
                relay_step(d - 1, q // 2)

    @pl.loop(0, HH)
    def _(f):
        relay_step(Z - 1, f)

    @pl.loop(0, Z)
    def _(zp):
        @pl.loop(0, H)
        def _(q):
            sibling(zp, q, 1 - k).wait_recv()

            @pl.when(jnp.logical_not(diag) & jnp.logical_not(relays(q // 2)))
            def _():
                relay(zp, q % 2, q // 2).wait_recv()

    half = pl.ds(pl.multiple_of(k * (N // 2), N // 2), N // 2)

    @pl.when(diag)
    def _():
        cp = pltpu.make_async_copy(obuf.at[:, half], cbuf, loc_s)
        cp.start()
        cp.wait()

    acp.wait()
    for o in range(1, R):
        acopy(o).wait_recv()

    def pair(t):
        return pltpu.make_async_remote_copy(
            sout.at[t], sin.at[t], pair_s.at[t], pair_r.at[t], device_id=(r, sib), device_id_type=MESH)

    def prefix(t):
        return pltpu.make_async_remote_copy(
            upout.at[t], upin.at[t], pre_s.at[t], pre_r.at[t], device_id=(r, c + 2), device_id_type=MESH)

    def suffix(t):
        return pltpu.make_async_remote_copy(
            dnout.at[t], dnin.at[t], suf_s.at[t], suf_r.at[t], device_id=(r, c - 2), device_id_type=MESH)

    def share(t, kk):
        ref = tot.at[t, :, pl.ds(pl.multiple_of(kk * W, W), W)]
        return pltpu.make_async_remote_copy(
            ref, ref, tot_s.at[t], tot_r.at[t], device_id=(r, sib), device_id_type=MESH)

    def project(t):
        ktile(t).wait()
        mu = pl.ds(pl.multiple_of(t * T, T), T)
        total = jnp.zeros((abuf.shape[0], T), jnp.float32)
        for n in range(NU // S):
            nu = pl.ds(n * S, S)
            dens = jnp.zeros((S, T), jnp.float32)
            for zp in range(Z):
                dens += lax.dot_general(cbuf[zp, nu], obuf[zp, mu], (((1,), (1,)), ((), ())),
                                        preferred_element_type=jnp.float32)
            w = (dens * kbuf[t % KS, nu].astype(jnp.float32)).astype(jnp.bfloat16)
            total += jnp.dot(abuf[:, nu], w, preferred_element_type=jnp.float32)
        first, second = total[:, :W], total[:, W:]
        pown[t] = jnp.where(k == 0, first, second)
        sout[t] = jnp.where(k == 0, second, first).astype(jnp.bfloat16)
        pair(t).start()

        @pl.when(t + KS < NT)
        def _():
            ktile(t + KS).start()

    far = jnp.maximum(z, Z - 1 - z)

    @pl.loop(0, NT + Z + 1)
    def _(s):
        @pl.when(s < NT)
        def _():
            project(s)

        t_pair = s - 1

        @pl.when((t_pair >= 0) & (t_pair < NT))
        def _():
            pair(t_pair).wait_recv()
            pown[t_pair] += sin[t_pair].astype(jnp.float32)

        t_up = s - 1 - z

        @pl.when((t_up >= 0) & (t_up < NT))
        def _():
            @pl.when(z > 0)
            def _():
                prefix(t_up).wait_recv()

            @pl.when(z < Z - 1)
            def _():
                upout[t_up] = (pown[t_up] + upin[t_up].astype(jnp.float32)).astype(jnp.bfloat16)
                prefix(t_up).start()

        t_dn = s - 1 - (Z - 1 - z)

        @pl.when((t_dn >= 0) & (t_dn < NT))
        def _():
            @pl.when(z < Z - 1)
            def _():
                suffix(t_dn).wait_recv()

            @pl.when(z > 0)
            def _():
                dnout[t_dn] = (pown[t_dn] + dnin[t_dn].astype(jnp.float32)).astype(jnp.bfloat16)
                suffix(t_dn).start()

        t_tot = s - 1 - far

        @pl.when((t_tot >= 0) & (t_tot < NT))
        def _():
            tot[t_tot, :, pl.ds(pl.multiple_of(k * W, W), W)] = (
                pown[t_tot] + upin[t_tot].astype(jnp.float32) + dnin[t_tot].astype(jnp.float32)
            ).astype(jnp.bfloat16)
            share(t_tot, k).start()

        t_ex = s - 2 - far

        @pl.when((t_ex >= 0) & (t_ex < NT))
        def _():
            share(t_ex, 1 - k).wait_recv()

            @pl.when(t_ex == 0)
            def _():
                fcopy.wait()
            acc[...] += jnp.dot(
                tot[t_ex], fbuf[pl.ds(pl.multiple_of(t_ex * T, T), T)], preferred_element_type=jnp.float32)

    def quarter(o):
        return pltpu.make_async_remote_copy(
            rout.at[o - 1], rin.at[o - 1], red_s.at[o - 1], red_r.at[o - 1],
            device_id=((r + o) % R, c), device_id_type=MESH)

    def rows_of(rr):
        return pl.ds(pl.multiple_of(rr * J, J), J)

    for o in (2, 1, 3)[: R - 1]:
        rout[o - 1] = acc[rows_of((r + o) % R)].astype(jnp.bfloat16)
        quarter(o).start()
    result = acc[rows_of(r)]
    for o in range(1, R):
        quarter(o).wait_recv()
        result += rin[o - 1].astype(jnp.float32)
    out[...] = (-result).astype(jnp.bfloat16)

    for o in range(1, R):
        acopy(o).wait_send()
        quarter(o).wait_send()

    @pl.loop(0, NT)
    def _(t):
        pair(t).wait_send()
        share(t, k).wait_send()

        @pl.when(z < Z - 1)
        def _():
            prefix(t).wait_send()

        @pl.when(z > 0)
        def _():
            suffix(t).wait_send()

    @pl.loop(0, Z)
    def _(zp):
        @pl.loop(0, H)
        def _(q):
            @pl.when((zp <= z) & (z < Z - 1))
            def _():
                line(zp, q, True).wait_send()

            @pl.when((zp >= z) & (z > 0))
            def _():
                line(zp, q, False).wait_send()

            sibling(zp, q, k).wait_send()

            @pl.when(diag)
            def _():
                from_diag(zp, q).wait_send()

            @pl.when(jnp.logical_not(diag) & relays(q // 2))
            def _():
                relay(zp, q % 2, q // 2).wait_send()


def relayed(R, C, orbitals, kernel, applied, fit):
    Z = C // 2
    N, B = orbitals.shape
    NU, M = kernel.shape
    G = fit.shape[1]
    at = applied.T
    J = at.shape[0]
    NT = M // T
    W = T // 2
    dma = pltpu.SemaphoreType.DMA
    low, high = jnp.bfloat16, jnp.float32
    tiles = pltpu.VMEM((NT, R * J, W), low)
    return pl.pallas_call(
        functools.partial(whole_kernel, R, C),
        out_shape=jax.ShapeDtypeStruct((J, G), low),
        in_specs=[pl.BlockSpec(memory_space=pl.ANY)] * 4,
        out_specs=pl.BlockSpec(memory_space=pltpu.VMEM),
        scratch_shapes=[
            pltpu.VMEM((Z, N, 2 * B), low),
            pltpu.VMEM((Z, NU, 2 * B), low),
            pltpu.VMEM((R * J, NU), low),
            pltpu.VMEM((KS, NU, T), low),
            pltpu.VMEM((M, G), low),
            pltpu.VMEM((NT, R * J, W), high),
            tiles, tiles, tiles, tiles, tiles, tiles,
            pltpu.VMEM((NT, R * J, T), low),
            pltpu.VMEM((R * J, G), high),
            pltpu.VMEM((R - 1, J, G), low),
            pltpu.VMEM((R - 1, J, G), low),
            dma, dma((KS,)), dma,
            dma((Z, H)), dma((Z, H)), dma((Z, H)), dma((Z, H)),
            dma((Z, H)), dma((Z, H)), dma((Z, 2, H // 2)),
            dma((R,)), dma((R,)),
        ] + [dma((NT,))] * 8 + [dma((R - 1,))] * 2,
        compiler_params=pltpu.CompilerParams(
            collective_id=0, has_side_effects=True, vmem_limit_bytes=60 * 1024 * 1024),
    )(orbitals, at, kernel, fit)


def plain(orbitals, kernel, applied, fit):
    columns = lax.all_gather(orbitals, "row", axis=0, tiled=True)
    nearby = lax.all_to_all(columns, "col", split_axis=0, concat_axis=1, tiled=True)
    density = lax.dot_general(
        nearby,
        lax.all_gather(orbitals, "col", axis=1, tiled=True),
        (((1,), (1,)), ((), ())),
        preferred_element_type=jnp.float32,
    )
    weighted = (density * kernel.astype(jnp.float32)).astype(jnp.bfloat16)
    partial_sum = lax.dot_general(
        weighted,
        lax.all_gather(applied, "row", axis=1, tiled=True),
        (((0,), (0,)), ((), ())),
        preferred_element_type=jnp.float32,
    )
    projected = lax.psum(partial_sum, "col")
    projected_low = projected.astype(jnp.bfloat16)
    result = lax.psum_scatter(
        -lax.dot_general(
            projected_low, fit, (((0,), (0,)), ((), ())), preferred_element_type=jnp.float32
        ),
        "row",
        scatter_dimension=0,
        tiled=True,
    )
    return result.astype(jnp.bfloat16)


def solution(mesh):
    R, C = mesh.shape["row"], mesh.shape["col"]

    def per_device(orbitals, kernel, applied, fit):
        if R == 4 and C == 2 * R and orbitals.shape[1] % 128 == 0:
            return relayed(R, C, orbitals, kernel, applied, fit)
        return plain(orbitals, kernel, applied, fit)

    return jax.shard_map(
        per_device,
        mesh=mesh,
        in_specs=(P("row", "col"), P("col", "row"), P("col", "row"), P("row", "col")),
        out_specs=P("row", "col"),
        check_vma=False,
    )
```
